32 devices in a mesh: groups: 2 (over x), lat: 16 (over z, y, core).
Axes of the slice: x: 2, y: 2, z: 4, core: 2. Of those that a mesh axis runs over, the one named last changes fastest.
Arguments:
- mesh_latent: bfloat16 [40960, 512], P(('groups', 'lat')), parts along dimension 0, may hold values from -6 to 6
- grid_latent: bfloat16 [32768, 512], P(('groups', 'lat')), parts along dimension 0, may hold values from -6 to 6
- near_senders: int32 [32, 5, 512], P(('groups', 'lat')), parts along dimension 0, may hold values from 0 to 1279
- near_receivers: int32 [32, 5, 512], P(('groups', 'lat')), parts along dimension 0, may hold values from 0 to 1279
- near_counts: int32 [32, 5], P(('groups', 'lat')), parts along dimension 0, may hold values from 0 to 512, as said below
- near_geom: bfloat16 [32, 4, 2560], P(('groups', 'lat')), parts along dimension 0, may hold values from -6 to 6
- far_senders: int32 [32, 16, 2], P(('groups', 'lat')), parts along dimension 0, may hold values from 0 to 7
- far_receivers: int32 [32, 16, 2], P(('groups', 'lat')), parts along dimension 0, may hold values from 0 to 1279
- far_counts: int32 [32, 16], P(('groups', 'lat')), parts along dimension 0, may hold values from 0 to 2, as said below
- far_geom: bfloat16 [32, 4, 32], P(('groups', 'lat')), parts along dimension 0, may hold values from -6 to 6
- dec_senders: int32 [3, 32768], P(None, ('groups', 'lat')), parts along dimension 1, may hold values from 0 to 3839, as said below
- dec_geom: bfloat16 [4, 3, 32768], P(None, None, ('groups', 'lat')), parts along dimension 2, may hold values from -6 to 6
- edge_weights: bfloat16 [2, 3, 512, 512], replicated, may hold values from -0.25 to 0.25
- node_weights: bfloat16 [2, 3, 512, 512], replicated, may hold values from -0.1875 to 0.1875
- geom_weights: bfloat16 [2, 4, 512], replicated, may hold values from -3 to 3
- biases: float32 [4, 3, 512], replicated, may hold values from -3 to 3
- gains: float32 [4, 512], replicated, may hold values from 0.25 to 1.75
Outputs:
- mesh_out: bfloat16 [40960, 512], P(('groups', 'lat')), parts along dimension 0
- grid_out: bfloat16 [32768, 512], P(('groups', 'lat')), parts along dimension 0
The draws below stay inside these ranges and needn't reach their ends.
There are 2 independent parts, one for each index of `groups`. The reference program is written for one: setup_inputs(seed, part) draws one part's arguments, and reference() takes and returns one part's arrays. A program takes and returns all parts, laid end to end along the dimension named above; an argument that names none is the same for every part. Nothing has to cross between parts.
Inputs may be any that keep to these rules, and one draw needn't show every extreme that they name: `near_counts`: A block of a source band outside 0..15 holds no live slot. Otherwise the block of the band itself holds 384 to 512 live slots, a block one band away 512 // 4 to 256, a block two bands away 512 // 8 to 128; each of these most is reached by some band in every draw. `far_counts`: every receiving band has at least one block with 2 live slots. `dec_senders`: A grid node of band b names mesh node (b - 1) * 1280 + value; on band 0 values are 1280 or more, on band 16 - 1 below 2560.
All inputs are finite; a program needn't handle non-finite values.
Results may differ from the reference program's by a relative error of at most 0.006.
Values may be sent and summed in bfloat16 or wider, within the bound.
A program may use at most 128 MiB of HBM per device.

```python
import jax
import jax.numpy as jnp
from jax import lax

L = 512
M_DEV = 1280
G_DEV = 1024
NEAR_CAP = 512
FAR_CAP = 2
HOT = 8
REACH = 2
EDGE_FEATS = 4
WINDOW = 5
BANDS = 16
MESH = 20480
GRID = 16384


def draw_near_counts(key, part):
    key = jax.random.fold_in(key, 5)
    keys = jax.random.split(key, 2)
    shape = (BANDS, WINDOW)
    band_rows = lax.broadcasted_iota(jnp.int32, shape, 0)
    offsets = lax.broadcasted_iota(jnp.int32, shape, 1) - REACH
    distance = jnp.abs(offsets)
    lowest = jnp.where(distance == 0, NEAR_CAP * 3 // 4, jnp.where(distance == 1, NEAR_CAP // 4, NEAR_CAP // 8))
    highest = jnp.where(distance == 0, NEAR_CAP, jnp.where(distance == 1, NEAR_CAP // 2, NEAR_CAP // 4))
    counts = jax.random.randint(keys[0], shape, lowest, highest + 1)
    chosen = jax.random.randint(keys[1], (1, WINDOW), REACH, BANDS - REACH)
    counts = jnp.where(band_rows == chosen, highest, counts)
    source = band_rows + offsets
    return jnp.where((source >= 0) & (source < BANDS), counts, 0)


def draw_far_counts(key, part):
    key = jax.random.fold_in(key, 7)
    keys = jax.random.split(key, 2)
    draws = jax.random.randint(keys[0], (BANDS, BANDS), 0, 8)
    counts = jnp.clip(draws - 5, 0, FAR_CAP)
    full_column = jax.random.randint(keys[1], (BANDS, 1), 0, BANDS)
    columns = lax.broadcasted_iota(jnp.int32, (BANDS, BANDS), 1)
    return jnp.where(columns == full_column, FAR_CAP, counts)


def draw_dec_senders(key, part):
    key = jax.random.fold_in(key, 11)
    rows = lax.broadcasted_iota(jnp.int32, (3, GRID), 1)
    which = lax.broadcasted_iota(jnp.int32, (3, GRID), 0)
    band_number = rows // G_DEV
    lowest = jnp.where(band_number == 0, M_DEV, 0)
    highest = jnp.where(band_number == BANDS - 1, 2 * M_DEV, 3 * M_DEV)
    values = jax.random.randint(key, (3, GRID), lowest, highest)
    values = jnp.where((rows == G_DEV) & (which == 0), 3 * M_DEV - 1, values)
    values = jnp.where((rows == G_DEV + 1) & (which == 0), 0, values)
    return values


def plant(result, stream_key, smallest, top_value):
    dims = result.shape
    place = [jax.random.randint(jax.random.fold_in(stream_key, axis), (), 0, dims[axis]) for axis in range(len(dims))]
    result = result.at[tuple(place)].set(smallest)
    longest = dims.index(max(dims))
    place[longest] = (place[longest] + 1) % dims[longest]
    return result.at[tuple(place)].set(top_value)


def block_scale(stream_key, dims, shards, least, high):
    loudness = 1.0
    for dim, parts in shards:
        heights = jax.random.uniform(jax.random.fold_in(jax.random.fold_in(stream_key, 6), dim), (parts,), jnp.float32, least / len(shards), high / len(shards))
        loudness = loudness * jnp.repeat(jnp.exp(heights), dims[dim] // parts).reshape((-1,) + (1,) * (len(dims) - 1 - dim))
    return loudness


def gaussian(stream_key, shape, width, reach, cuts=(), kind=jnp.bfloat16):
    entries = jax.random.normal(stream_key, shape, jnp.float32) * width
    if len(cuts) > 0:
        entries = block_scale(stream_key, shape, cuts, -0.22, 0.18) * entries
    return jnp.clip(entries, min=-reach, max=reach).astype(kind)


def setup_inputs(seed: int = 0, part: int = 0) -> dict:
    arg_keys = jax.random.split(jax.random.key(seed), 18)
    part_keys = jax.random.split(jax.random.fold_in(arg_keys[17], part), 18)
    return {
        "mesh_latent": gaussian(part_keys[0], (MESH, L), 1.0, 6.0, ((0, 16),)),
        "grid_latent": gaussian(part_keys[1], (GRID, L), 1.0, 6.0, ((0, 16),)),
        "near_senders": plant(jax.random.randint(part_keys[2], (BANDS, WINDOW, NEAR_CAP), 0, M_DEV), jax.random.fold_in(part_keys[2], 1), 0, M_DEV - 1).astype(jnp.int32),
        "near_receivers": plant(jax.random.randint(part_keys[3], (BANDS, WINDOW, NEAR_CAP), 0, M_DEV), jax.random.fold_in(part_keys[3], 1), 0, M_DEV - 1).astype(jnp.int32),
        "near_counts": draw_near_counts(jax.random.fold_in(jax.random.fold_in(arg_keys[17], part), 71), part),
        "near_geom": gaussian(part_keys[5], (BANDS, EDGE_FEATS, WINDOW * NEAR_CAP), 1.0, 6.0, ((0, 16),)),
        "far_senders": plant(jax.random.randint(part_keys[6], (BANDS, BANDS, FAR_CAP), 0, HOT), jax.random.fold_in(part_keys[6], 1), 0, HOT - 1).astype(jnp.int32),
        "far_receivers": plant(jax.random.randint(part_keys[7], (BANDS, BANDS, FAR_CAP), 0, M_DEV), jax.random.fold_in(part_keys[7], 1), 0, M_DEV - 1).astype(jnp.int32),
        "far_counts": draw_far_counts(jax.random.fold_in(jax.random.fold_in(arg_keys[17], part), 71), part),
        "far_geom": gaussian(part_keys[9], (BANDS, EDGE_FEATS, BANDS * FAR_CAP), 1.0, 6.0, ((0, 16),)),
        "dec_senders": draw_dec_senders(jax.random.fold_in(jax.random.fold_in(arg_keys[17], part), 71), part),
        "dec_geom": gaussian(part_keys[11], (EDGE_FEATS, 3, GRID), 1.0, 6.0, ((2, 16),)),
        "edge_weights": gaussian(arg_keys[12], (2, 3, L, L), L ** -0.5, 0.25),
        "node_weights": gaussian(arg_keys[13], (2, 3, L, L), (2 * L) ** -0.5, 0.1875),
        "geom_weights": gaussian(arg_keys[14], (2, EDGE_FEATS, L), EDGE_FEATS ** -0.5, 3.0),
        "biases": gaussian(arg_keys[15], (4, 3, L), 0.5, 3.0, (), jnp.float32),
        "gains": jnp.clip(1.0 + 0.15 * jax.random.normal(arg_keys[16], (4, L), jnp.float32), 0.25, 1.75),
    }


EPSILON = 1e-05

def layer_norm(values, gain, shift):
    average = lax.optimization_barrier(jnp.mean(values, axis=-1, keepdims=True))
    centred = values - average
    variance = lax.optimization_barrier(jnp.mean(centred * centred, axis=-1, keepdims=True))
    return centred * lax.rsqrt(variance + EPSILON) * gain + shift

def matmul(left, right):
    return jnp.dot(left, right, preferred_element_type=jnp.float32)

def embed_geometry(geometry, weights):
    return jnp.einsum('kn,kl->nl', geometry.astype(jnp.float32), weights.astype(jnp.float32))

def edge_message(joined, out_weight, bias, gain):
    hidden = jax.nn.silu(joined + bias[0]).astype(jnp.bfloat16)
    output = matmul(hidden, out_weight) + bias[1]
    return layer_norm(output, gain, bias[2])

def node_update(latent, summed, weights, bias, gain):
    pre_act = matmul(latent, weights[0]) + matmul(summed.astype(jnp.bfloat16), weights[1]) + bias[0]
    hidden = jax.nn.silu(pre_act).astype(jnp.bfloat16)
    output = matmul(hidden, weights[2]) + bias[1]
    return (latent.astype(jnp.float32) + layer_norm(output, gain, bias[2])).astype(jnp.bfloat16)

def reference(mesh_latent, grid_latent, near_senders, near_receivers, near_counts, near_geom, far_senders, far_receivers, far_counts, far_geom, dec_senders, dec_geom, edge_weights, node_weights, geom_weights, biases, gains):
    latent_width = mesh_latent.shape[1]
    sent_all = matmul(mesh_latent, edge_weights[0, 0])
    recv_all = matmul(mesh_latent, edge_weights[0, 1]).reshape(BANDS, M_DEV, latent_width)
    window_offsets = jnp.arange(WINDOW, dtype=jnp.int32) - REACH
    band_starts = (jnp.arange(BANDS, dtype=jnp.int32) * M_DEV)[:, None]
    near_slots = jnp.arange(NEAR_CAP, dtype=jnp.int32)
    far_slots = jnp.arange(FAR_CAP, dtype=jnp.int32)

    def process_band(inputs):
        band_number, n_send, n_recv, n_count, n_geom, f_send, f_recv, f_count, f_geom, received_proj = inputs
        near_band = band_number + window_offsets
        near_source = jnp.clip(near_band[:, None] * M_DEV + n_send, 0, MESH - 1).reshape(-1)
        far_source = (band_starts + f_send).reshape(-1)
        source = jnp.concatenate([near_source, far_source]).astype(jnp.int32)
        target = jnp.concatenate([n_recv.reshape(-1), f_recv.reshape(-1)]).astype(jnp.int32)
        near_live = (near_slots[None, :] < n_count[:, None]).reshape(-1)
        far_live = (far_slots[None, :] < f_count[:, None]).reshape(-1)
        is_live = jnp.concatenate([near_live, far_live])
        geometry = jnp.concatenate([n_geom, f_geom], axis=1)
        joined = jnp.take(sent_all, source, axis=0) + jnp.take(received_proj, target, axis=0) + embed_geometry(geometry, geom_weights[0])
        message = edge_message(joined, edge_weights[0, 2], biases[0], gains[0])
        message = jnp.where(is_live[:, None], message, jnp.float32(0.0)).astype(jnp.bfloat16)
        return jax.ops.segment_sum(message.astype(jnp.float32), target, num_segments=M_DEV)
    band_ids = jnp.arange(BANDS, dtype=jnp.int32)
    summed = lax.map(process_band, (band_ids, near_senders, near_receivers, near_counts, near_geom, far_senders, far_receivers, far_counts, far_geom, recv_all)).reshape(MESH, latent_width)
    mesh_out = node_update(mesh_latent, summed, node_weights[0], biases[1], gains[1])
    sent_dec = matmul(mesh_out, edge_weights[1, 0])
    recv_dec = matmul(grid_latent, edge_weights[1, 1]).reshape(BANDS, G_DEV, latent_width)
    senders_banded = dec_senders.reshape(3, BANDS, G_DEV).transpose(1, 0, 2)
    geom_banded = dec_geom.reshape(EDGE_FEATS, 3, BANDS, G_DEV).transpose(2, 0, 1, 3)

    def decode_band(inputs):
        band_number, senders, geometry, received_proj = inputs
        source = (senders + (band_number - 1) * M_DEV).reshape(-1)
        sent_rows = jnp.take(sent_dec, source, axis=0).reshape(3, G_DEV, latent_width)
        geom_rows = embed_geometry(geometry.reshape(EDGE_FEATS, -1), geom_weights[1]).reshape(3, G_DEV, latent_width)
        joined = (sent_rows + received_proj[None] + geom_rows).reshape(3 * G_DEV, latent_width)
        message = edge_message(joined, edge_weights[1, 2], biases[2], gains[2])
        return lax.optimization_barrier(jnp.sum(message.reshape(3, G_DEV, latent_width), axis=0))
    summed_grid = lax.map(decode_band, (band_ids, senders_banded, geom_banded, recv_dec)).reshape(GRID, latent_width)
    grid_out = node_update(grid_latent, summed_grid, node_weights[1], biases[3], gains[3])
    return (mesh_out, grid_out)
```

```python
import functools

import jax
import jax.numpy as jnp
from jax import lax
from jax.experimental import pallas as pl
from jax.experimental.pallas import tpu as pltpu
from jax.sharding import PartitionSpec as P

EPSILON = 1e-05
MESH = pl.DeviceIdType.MESH
F32 = jnp.float32
BF16 = jnp.bfloat16
CHUNK = 256
HOT_ROWS = 16


def dot(left, right):
    return jnp.dot(left, right, preferred_element_type=F32)


def silu(value):
    half = 0.5 * value
    return half + half * jnp.tanh(half)


def layer_norm(values, gain, shift):
    average = jnp.mean(values, axis=-1, keepdims=True)
    centred = values - average
    variance = jnp.mean(centred * centred, axis=-1, keepdims=True)
    return centred * lax.rsqrt(variance + EPSILON) * gain + shift


def one_hot(column, first, count):
    ids = lax.broadcasted_iota(jnp.int32, (column.shape[0], count), 1) + first
    return jnp.where(ids == column, 1.0, 0.0).astype(BF16)


def kernel(
    n, caps,
    latent, near_send, idx_rows, geo_rows, dec_rows, dec_geo, geom_w, biases, gains,
    grid_hbm, ew_hbm, nw_hbm,
    mesh_hbm, grid_out_hbm,
    ew, nw, grid, idx_in, served, sent, hot, cols, geo_cols, dec_cols, dec_geo_cols,
    pre_edge, msg, pre_node, mout, win, acc, pre_grid, pre_gnode, gout,
    load_sem, idx_send, idx_recv, row_send, row_recv, hot_send, hot_recv,
    halo_send, halo_recv, out_sem, gout_sem,
):
    me = lax.axis_index("lat")
    rows = latent.shape[0]
    grid_rows = grid.shape[0]
    edges = idx_rows.shape[1]
    near_edges = sum(cap for _, cap in caps)
    own = caps[0][1]
    far_edges = edges - near_edges

    def peer(by):
        return {"lat": lax.rem(me + by + 2 * n, n)}

    loads = [
        pltpu.make_async_copy(ew_hbm, ew, load_sem.at[0]),
        pltpu.make_async_copy(nw_hbm, nw, load_sem.at[1]),
        pltpu.make_async_copy(grid_hbm, grid, load_sem.at[2]),
    ]
    for load in loads:
        load.start()

    barrier = pltpu.get_barrier_semaphore()

    @pl.loop(1, n)
    def _(k):
        pl.semaphore_signal(barrier, inc=1, device_id=peer(k), device_id_type=MESH)

    pl.semaphore_wait(barrier, n - 1)

    requests = []
    starts, at = ({}, 0)
    for j, cap in caps:
        starts[j] = at
        at += cap
    for slot, (j, cap) in enumerate(caps[1:]):
        requests.append(pltpu.make_async_remote_copy(
            src_ref=near_send, dst_ref=idx_in.at[slot],
            send_sem=idx_send.at[slot], recv_sem=idx_recv.at[slot],
            device_id=peer(j - 2), device_id_type=MESH,
        ))
        requests[-1].start()

    def hot_copy(k):
        return pltpu.make_async_remote_copy(
            src_ref=latent.at[pl.ds(0, HOT_ROWS)],
            dst_ref=hot.at[pl.ds(pl.multiple_of(me * HOT_ROWS, HOT_ROWS), HOT_ROWS)],
            send_sem=hot_send.at[k], recv_sem=hot_recv.at[k],
            device_id=peer(k), device_id_type=MESH,
        )

    @pl.loop(1, n)
    def _(k):
        hot_copy(k).start()

    hot[pl.ds(pl.multiple_of(me * HOT_ROWS, HOT_ROWS), HOT_ROWS), :] = latent[0:HOT_ROWS, :]

    cols[...] = jnp.transpose(idx_rows[...])
    geo_cols[...] = jnp.transpose(geo_rows[...])

    replies = []
    for slot, (j, cap) in enumerate(caps[1:]):
        requests[slot].wait_recv()
        wanted = jnp.transpose(jnp.broadcast_to(idx_in[slot, j:j + 1, :cap], (8, cap)))
        place = starts[j] - own
        served[place:place + cap, :] = dot(
            one_hot(wanted[:, 0:1], 0, rows), latent[...]).astype(BF16)
        replies.append(pltpu.make_async_remote_copy(
            src_ref=served.at[pl.ds(place, cap)],
            dst_ref=sent.at[pl.ds(place, cap)],
            send_sem=row_send.at[slot], recv_sem=row_recv.at[slot],
            device_id=peer(2 - j), device_id_type=MESH,
        ))
        replies[-1].start()

    loads[0].wait()
    loads[1].wait()

    def received(start, count):
        here = pl.ds(start, count)
        picked = dot(one_hot(cols[here, 0:1], 0, rows), latent[...]).astype(BF16)
        pre_edge[here, :] = (
            dot(picked, ew[0, 1])
            + dot(geo_cols[here, :].astype(BF16), geom_w[0])
            + biases[0, 0:1, :]
        )

    def message(sent_rows, start, count):
        here = pl.ds(start, count)
        hidden = silu(dot(sent_rows, ew[0, 0]) + pre_edge[here, :]).astype(BF16)
        output = dot(hidden, ew[0, 2]) + biases[0, 1:2, :]
        msg[here, :] = layer_norm(output, gains[0:1, :], biases[0, 2:3, :]).astype(BF16)

    @pl.loop(0, near_edges // CHUNK)
    def _(c):
        received(pl.multiple_of(c * CHUNK, CHUNK), CHUNK)

    received(near_edges, far_edges)

    @pl.loop(0, own // CHUNK)
    def _(c):
        start = pl.multiple_of(c * CHUNK, CHUNK)
        picked = dot(one_hot(cols[pl.ds(start, CHUNK), 1:2], 0, rows), latent[...])
        message(picked.astype(BF16), start, CHUNK)

    @pl.loop(0, rows // CHUNK)
    def _(c):
        here = pl.ds(pl.multiple_of(c * CHUNK, CHUNK), CHUNK)
        pre_node[here, :] = dot(latent[here, :], nw[0, 0]) + biases[1, 0:1, :]

    @pl.loop(1, n)
    def _(k):
        hot_copy(k).wait_recv()

    hot_rows = dot(one_hot(cols[near_edges:edges, 1:2], 0, n * HOT_ROWS), hot[...])
    message(hot_rows.astype(BF16), near_edges, far_edges)

    for reply in replies:
        reply.wait_recv()

    @pl.loop(0, (near_edges - own) // CHUNK)
    def _(c):
        start = pl.multiple_of(c * CHUNK, CHUNK)
        message(sent[pl.ds(start, CHUNK), :], pl.multiple_of(own + start, CHUNK), CHUNK)

    def halo_copy(side, c):
        here = pl.ds(pl.multiple_of(c * CHUNK, CHUNK), CHUNK)
        return pltpu.make_async_remote_copy(
            src_ref=mout.at[here], dst_ref=win.at[side, here],
            send_sem=halo_send.at[side, c], recv_sem=halo_recv.at[side, c],
            device_id=peer(1 - 2 * side), device_id_type=MESH,
        )

    @pl.loop(0, rows // CHUNK)
    def _(c):
        first = pl.multiple_of(c * CHUNK, CHUNK)
        here = pl.ds(first, CHUNK)
        ids = lax.broadcasted_iota(jnp.int32, (CHUNK, edges), 0) + first
        selector = jnp.where(ids == idx_rows[2:3, :], 1.0, 0.0).astype(BF16)
        summed = dot(selector, msg[...]).astype(BF16)
        hidden = silu(pre_node[here, :] + dot(summed, nw[0, 1])).astype(BF16)
        output = dot(hidden, nw[0, 2]) + biases[1, 1:2, :]
        updated = layer_norm(output, gains[1:2, :], biases[1, 2:3, :])
        mout[here, :] = (latent[here, :].astype(F32) + updated).astype(BF16)
        halo_copy(0, c).start()
        halo_copy(1, c).start()

    store_mesh = pltpu.make_async_copy(mout, mesh_hbm, out_sem)
    store_mesh.start()

    dec_cols[...] = jnp.transpose(dec_rows[...])
    for k in range(3):
        dec_geo_cols[k] = jnp.transpose(dec_geo[k])
    loads[2].wait()

    @pl.loop(0, grid_rows // CHUNK)
    def _(c):
        here = pl.ds(pl.multiple_of(c * CHUNK, CHUNK), CHUNK)
        latents = grid[here, :]
        pre_grid[here, :] = dot(latents, ew[1, 1]) + biases[2, 0:1, :]
        pre_gnode[here, :] = dot(latents, nw[1, 0]) + biases[3, 0:1, :]
        for k in range(3):
            acc[k, here, :] = dot(
                one_hot(dec_cols[here, k:k + 1], rows, rows), mout[...]).astype(BF16)

    chunks = rows // CHUNK
    early = (chunks + 1) // 2 * CHUNK

    def neighbours(column, first, count):
        return (
            dot(one_hot(column, first, count), win[0, first:first + count, :])
            + dot(one_hot(column, 2 * rows + first, count), win[1, first:first + count, :])
        )

    for c in range(early // CHUNK):
        halo_copy(0, c).wait_recv()
        halo_copy(1, c).wait_recv()

    @pl.loop(0, grid_rows // CHUNK)
    def _(c):
        here = pl.ds(pl.multiple_of(c * CHUNK, CHUNK), CHUNK)
        for k in range(3):
            acc[k, here, :] = (
                acc[k, here, :].astype(F32) + neighbours(dec_cols[here, k:k + 1], 0, early)
            ).astype(BF16)

    for c in range(early // CHUNK, chunks):
        halo_copy(0, c).wait_recv()
        halo_copy(1, c).wait_recv()

    def store_grid(c):
        here = pl.ds(pl.multiple_of(c * CHUNK, CHUNK), CHUNK)
        return pltpu.make_async_copy(gout.at[here], grid_out_hbm.at[here], gout_sem.at[c])

    @pl.loop(0, grid_rows // CHUNK)
    def _(c):
        here = pl.ds(pl.multiple_of(c * CHUNK, CHUNK), CHUNK)
        total = jnp.zeros((CHUNK, latent.shape[1]), F32)
        for k in range(3):
            picked = (
                acc[k, here, :].astype(F32)
                + neighbours(dec_cols[here, k:k + 1], early, rows - early)
            ).astype(BF16)
            pre = (
                dot(picked, ew[1, 0]) + pre_grid[here, :]
                + dot(dec_geo_cols[k, here, :].astype(BF16), geom_w[1])
            )
            output = dot(silu(pre).astype(BF16), ew[1, 2]) + biases[2, 1:2, :]
            total += layer_norm(output, gains[2:3, :], biases[2, 2:3, :])
        hidden = silu(pre_gnode[here, :] + dot(total.astype(BF16), nw[1, 1])).astype(BF16)
        output = dot(hidden, nw[1, 2]) + biases[3, 1:2, :]
        updated = layer_norm(output, gains[3:4, :], biases[3, 2:3, :])
        gout[here, :] = (grid[here, :].astype(F32) + updated).astype(BF16)
        store_grid(c).start()

    for c in range(grid_rows // CHUNK):
        store_grid(c).wait()
    store_mesh.wait()
    for request in requests:
        request.wait_send()
    for reply in replies:
        reply.wait_send()

    @pl.loop(1, n)
    def _(k):
        hot_copy(k).wait_send()

    for c in range(chunks):
        halo_copy(0, c).wait_send()
        halo_copy(1, c).wait_send()


def pad_rows(value, count):
    return jnp.pad(value, ((0, count - value.shape[0]),) + ((0, 0),) * (value.ndim - 1))


def local(
    mesh_latent, grid_latent, near_senders, near_receivers, near_counts, near_geom,
    far_senders, far_receivers, far_counts, far_geom, dec_senders, dec_geom,
    edge_weights, node_weights, geom_weights, biases, gains,
):
    n = lax.axis_size("lat")
    rows, width = mesh_latent.shape
    grid_rows = grid_latent.shape[0]
    cap = near_senders.shape[2]
    caps = ((2, cap), (1, cap // 2), (3, cap // 2), (0, cap // 4), (4, cap // 4))
    far_slots = far_senders.shape[1] * far_senders.shape[2]
    far_padded = -(-far_slots // 128) * 128

    def joined(near, far, fill=0):
        far = jnp.pad(far.reshape(-1), (0, far_padded - far_slots), constant_values=fill)
        return jnp.concatenate([near[j, :c] for j, c in caps] + [far])

    near_live = lax.broadcasted_iota(jnp.int32, near_senders.shape[1:], 1) < near_counts[0][:, None]
    far_live = lax.broadcasted_iota(jnp.int32, far_senders.shape[1:], 1) < far_counts[0][:, None]
    hot_index = far_senders[0] + HOT_ROWS * lax.broadcasted_iota(jnp.int32, far_senders.shape[1:], 0)
    idx_rows = pad_rows(jnp.stack([
        joined(near_receivers[0], far_receivers[0]),
        joined(near_senders[0], hot_index),
        joined(
            jnp.where(near_live, near_receivers[0], -1),
            jnp.where(far_live, far_receivers[0], -1), -1,
        ),
    ]), 8)
    near_geo = near_geom[0].reshape(4, 5, cap)
    geo_rows = pad_rows(jnp.concatenate(
        [near_geo[:, j, :c] for j, c in caps]
        + [jnp.pad(far_geom[0], ((0, 0), (0, far_padded - far_slots)))], axis=1,
    ).astype(F32), 8)
    edges = idx_rows.shape[1]
    remote = sum(c for _, c in caps[1:])
    dec_rows = pad_rows(dec_senders, 8)
    dec_geo = jnp.pad(dec_geom.transpose(1, 0, 2).astype(F32), ((0, 0), (0, 4), (0, 0)))
    geom_w = jnp.pad(geom_weights, ((0, 0), (0, 4), (0, 0)))
    chunks = rows // CHUNK

    vmem = pl.BlockSpec(memory_space=pltpu.VMEM)
    hbm = pl.BlockSpec(memory_space=pl.ANY)
    dma = pltpu.SemaphoreType.DMA
    return pl.pallas_call(
        functools.partial(kernel, n, caps),
        out_shape=(
            jax.ShapeDtypeStruct((rows, width), BF16),
            jax.ShapeDtypeStruct((grid_rows, width), BF16),
        ),
        in_specs=[vmem] * 9 + [hbm] * 3,
        out_specs=(hbm, hbm),
        scratch_shapes=[
            pltpu.VMEM(edge_weights.shape, BF16),
            pltpu.VMEM(node_weights.shape, BF16),
            pltpu.VMEM((grid_rows, width), BF16),
            pltpu.VMEM((4, 5, cap), jnp.int32),
            pltpu.VMEM((remote, width), BF16),
            pltpu.VMEM((remote, width), BF16),
            pltpu.VMEM((n * HOT_ROWS, width), BF16),
            pltpu.VMEM((edges, 8), jnp.int32),
            pltpu.VMEM((edges, 8), F32),
            pltpu.VMEM((grid_rows, 8), jnp.int32),
            pltpu.VMEM((3, grid_rows, 8), F32),
            pltpu.VMEM((edges, width), F32),
            pltpu.VMEM((edges, width), BF16),
            pltpu.VMEM((rows, width), F32),
            pltpu.VMEM((rows, width), BF16),
            pltpu.VMEM((2, rows, width), BF16),
            pltpu.VMEM((3, grid_rows, width), BF16),
            pltpu.VMEM((grid_rows, width), F32),
            pltpu.VMEM((grid_rows, width), F32),
            pltpu.VMEM((grid_rows, width), BF16),
            dma((3,)), dma((4,)), dma((4,)), dma((4,)), dma((4,)), dma((n,)), dma((n,)),
            dma((2, chunks)), dma((2, chunks)), dma, dma((grid_rows // CHUNK,)),
        ],
        compiler_params=pltpu.CompilerParams(
            collective_id=0, has_side_effects=True, vmem_limit_bytes=56 * 2**20,
        ),
        cost_estimate=pl.CostEstimate(flops=40_000_000_000, bytes_accessed=16_000_000, transcendentals=4_000_000),
    )(
        mesh_latent, near_senders[0], idx_rows, geo_rows, dec_rows, dec_geo, geom_w, biases, gains,
        grid_latent, edge_weights, node_weights,
    )


def solution(mesh):
    return jax.shard_map(
        local,
        mesh=mesh,
        in_specs=(
            P(("groups", "lat"), None),
            P(("groups", "lat"), None),
            P(("groups", "lat"), None, None),
            P(("groups", "lat"), None, None),
            P(("groups", "lat"), None),
            P(("groups", "lat"), None, None),
            P(("groups", "lat"), None, None),
            P(("groups", "lat"), None, None),
            P(("groups", "lat"), None),
            P(("groups", "lat"), None, None),
            P(None, ("groups", "lat")),
            P(None, None, ("groups", "lat")),
            P(),
            P(),
            P(),
            P(),
            P(),
        ),
        out_specs=(P(("groups", "lat"), None), P(("groups", "lat"), None)),
        check_vma=False,
    )
```

```python
import functools

import jax
import jax.numpy as jnp
from jax import lax
from jax.experimental import pallas as pl
from jax.experimental.pallas import tpu as pltpu
from jax.sharding import PartitionSpec as P

EPSILON = 1e-05
MESH = pl.DeviceIdType.MESH
F32 = jnp.float32
BF16 = jnp.bfloat16
CHUNK = 256
HOT_ROWS = 16


def dot(left, right):
    return jnp.dot(left, right, preferred_element_type=F32)


def silu(value):
    half = 0.5 * value
    return half + half * jnp.tanh(half)


def layer_norm(values, gain, shift):
    average = jnp.mean(values, axis=-1, keepdims=True)
    centred = values - average
    variance = jnp.mean(centred * centred, axis=-1, keepdims=True)
    return centred * lax.rsqrt(variance + EPSILON) * gain + shift


def one_hot(column, first, count):
    ids = lax.broadcasted_iota(jnp.int32, (column.shape[0], count), 1) + first
    return jnp.where(ids == column, 1.0, 0.0).astype(BF16)


def kernel(
    n, caps, far_cap,
    latent_hbm, grid_hbm, send_hbm, recv_hbm, counts_hbm, geom_hbm,
    far_send_hbm, far_recv_hbm, far_counts_hbm, far_geom_hbm,
    dec_send_hbm, dec_geom_hbm, ew_hbm, nw_hbm, geom_w_hbm, biases_hbm, gains_hbm,
    mesh_hbm, grid_out_hbm,
    latent, near_recv, near_send, counts, near_geom, far_send, far_recv, far_counts, far_geom,
    dec_send, dec_geom, geom_raw, biases, gains,
    idx_rows, geo_rows, dec_rows, dec_geo_rows, geom_w,
    ew, nw, grid, idx_in, served, sent, hot, cols, geo_cols, dec_cols, dec_geo_cols,
    pre_edge, msg, pre_node, mout, win, acc, pre_grid, pre_gnode, gout,
    load_sem, idx_send, idx_recv, row_send, row_recv, hot_send, hot_recv,
    halo_send, halo_recv, out_sem, gout_sem,
):
    me = lax.axis_index("lat")
    rows = latent.shape[0]
    grid_rows = grid.shape[0]
    edges = idx_rows.shape[1]
    near_edges = sum(cap for _, cap in caps)
    own = caps[0][1]
    far_edges = edges - near_edges

    def peer(by):
        return {"lat": lax.rem(me + by + 2 * n, n)}

    barrier = pltpu.get_barrier_semaphore()

    @pl.loop(1, n)
    def _(k):
        pl.semaphore_signal(barrier, inc=1, device_id=peer(k), device_id_type=MESH)

    pairs = (
        (latent_hbm, latent), (send_hbm, near_send), (recv_hbm, near_recv), (counts_hbm, counts),
        (geom_hbm, near_geom), (far_send_hbm, far_send), (far_recv_hbm, far_recv),
        (far_counts_hbm, far_counts), (far_geom_hbm, far_geom), (dec_send_hbm, dec_send),
        (dec_geom_hbm, dec_geom), (geom_w_hbm, geom_raw), (biases_hbm, biases), (gains_hbm, gains),
        (ew_hbm, ew), (nw_hbm, nw), (grid_hbm, grid),
    )
    loads = [
        pltpu.make_async_copy(source, target, load_sem.at[i])
        for i, (source, target) in enumerate(pairs)
    ]
    for load in loads:
        load.start()

    starts, at = ({}, 0)
    for j, cap in caps:
        starts[j] = at
        at += cap
    idx_rows[...] = jnp.zeros_like(idx_rows)
    idx_rows[2:3, :] = jnp.full((1, edges), -1, jnp.int32)
    geo_rows[...] = jnp.zeros_like(geo_rows)
    dec_rows[...] = jnp.zeros_like(dec_rows)
    dec_geo_rows[...] = jnp.zeros_like(dec_geo_rows)
    geom_w[...] = jnp.zeros_like(geom_w)

    pl.semaphore_wait(barrier, n - 1)

    requests = []
    for slot, (j, cap) in enumerate(caps[1:]):
        requests.append(pltpu.make_async_remote_copy(
            src_ref=send_hbm, dst_ref=idx_in.at[slot],
            send_sem=idx_send.at[slot], recv_sem=idx_recv.at[slot],
            device_id=peer(j - 2), device_id_type=MESH,
        ))
        requests[-1].start()

    def hot_copy(k):
        return pltpu.make_async_remote_copy(
            src_ref=latent_hbm.at[pl.ds(0, HOT_ROWS)],
            dst_ref=hot.at[pl.ds(pl.multiple_of(me * HOT_ROWS, HOT_ROWS), HOT_ROWS)],
            send_sem=hot_send.at[k], recv_sem=hot_recv.at[k],
            device_id=peer(k), device_id_type=MESH,
        )

    @pl.loop(1, n)
    def _(k):
        hot_copy(k).start()

    for load in loads[:14]:
        load.wait()
    hot[pl.ds(pl.multiple_of(me * HOT_ROWS, HOT_ROWS), HOT_ROWS), :] = latent[0:HOT_ROWS, :]

    for j, cap in caps:
        here = slice(starts[j], starts[j] + cap)
        to = near_recv[j, :, :cap]
        live = lax.broadcasted_iota(jnp.int32, (1, cap), 1) < counts[0:1, j:j + 1]
        idx_rows[0:1, here] = to
        idx_rows[1:2, here] = near_send[j, :, :cap]
        idx_rows[2:3, here] = jnp.where(live, to, -1)
        first = j * near_recv.shape[2]
        geo_rows[0:4, here] = near_geom[:, first:first + cap].astype(F32)
    wide = far_edges // far_cap
    for c in range(far_cap):
        first = near_edges + c * wide
        here = slice(first, first + n)
        to = far_recv[c:c + 1, :]
        idx_rows[0:1, here] = to
        idx_rows[1:2, here] = far_send[c:c + 1, :] + HOT_ROWS * lax.broadcasted_iota(jnp.int32, (1, n), 1)
        idx_rows[2:3, here] = jnp.where(far_counts[0:1, :] > c, to, -1)
        place = lax.broadcasted_iota(jnp.int32, (far_cap * n, wide), 0)
        slots = far_cap * lax.broadcasted_iota(jnp.int32, (far_cap * n, wide), 1) + c
        geo_rows[0:4, first:first + wide] = dot(
            far_geom[...], jnp.where(place == slots, 1.0, 0.0).astype(BF16))
    geom_w[:, 0:4, :] = geom_raw[...].astype(F32)
    cols[...] = jnp.transpose(idx_rows[...])
    geo_cols[...] = jnp.transpose(geo_rows[...])

    replies = []
    for slot, (j, cap) in enumerate(caps[1:]):
        requests[slot].wait_recv()
        wanted = jnp.transpose(jnp.broadcast_to(idx_in[slot, j, :, :cap], (8, cap)))
        place = starts[j] - own
        served[place:place + cap, :] = dot(
            one_hot(wanted[:, 0:1], 0, rows), latent[...]).astype(BF16)
        replies.append(pltpu.make_async_remote_copy(
            src_ref=served.at[pl.ds(place, cap)],
            dst_ref=sent.at[pl.ds(place, cap)],
            send_sem=row_send.at[slot], recv_sem=row_recv.at[slot],
            device_id=peer(2 - j), device_id_type=MESH,
        ))
        replies[-1].start()

    loads[14].wait()
    loads[15].wait()

    def received(start, count):
        here = pl.ds(start, count)
        picked = dot(one_hot(cols[here, 0:1], 0, rows), latent[...]).astype(BF16)
        pre_edge[here, :] = (
            dot(picked, ew[0, 1])
            + dot(geo_cols[here, :].astype(BF16), geom_w[0].astype(BF16))
            + biases[0, 0:1, :]
        )

    def message(sent_rows, start, count):
        here = pl.ds(start, count)
        hidden = silu(dot(sent_rows, ew[0, 0]) + pre_edge[here, :]).astype(BF16)
        output = dot(hidden, ew[0, 2]) + biases[1, 0:1, :]
        msg[here, :] = layer_norm(output, gains[0:1, :], biases[2, 0:1, :]).astype(BF16)

    @pl.loop(0, near_edges // CHUNK)
    def _(c):
        received(pl.multiple_of(c * CHUNK, CHUNK), CHUNK)

    received(near_edges, far_edges)

    @pl.loop(0, own // CHUNK)
    def _(c):
        start = pl.multiple_of(c * CHUNK, CHUNK)
        picked = dot(one_hot(cols[pl.ds(start, CHUNK), 1:2], 0, rows), latent[...])
        message(picked.astype(BF16), start, CHUNK)

    @pl.loop(0, rows // CHUNK)
    def _(c):
        here = pl.ds(pl.multiple_of(c * CHUNK, CHUNK), CHUNK)
        pre_node[here, :] = dot(latent[here, :], nw[0, 0]) + biases[0, 1:2, :]

    @pl.loop(1, n)
    def _(k):
        hot_copy(k).wait_recv()

    hot_rows = dot(one_hot(cols[near_edges:edges, 1:2], 0, n * HOT_ROWS), hot[...])
    message(hot_rows.astype(BF16), near_edges, far_edges)

    for reply in replies:
        reply.wait_recv()

    @pl.loop(0, (near_edges - own) // CHUNK)
    def _(c):
        start = pl.multiple_of(c * CHUNK, CHUNK)
        message(sent[pl.ds(start, CHUNK), :], pl.multiple_of(own + start, CHUNK), CHUNK)

    def halo_copy(side, c):
        here = pl.ds(pl.multiple_of(c * CHUNK, CHUNK), CHUNK)
        return pltpu.make_async_remote_copy(
            src_ref=mout.at[here], dst_ref=win.at[side, here],
            send_sem=halo_send.at[side, c], recv_sem=halo_recv.at[side, c],
            device_id=peer(1 - 2 * side), device_id_type=MESH,
        )

    @pl.loop(0, rows // CHUNK)
    def _(c):
        first = pl.multiple_of(c * CHUNK, CHUNK)
        here = pl.ds(first, CHUNK)
        ids = lax.broadcasted_iota(jnp.int32, (CHUNK, edges), 0) + first
        selector = jnp.where(ids == idx_rows[2:3, :], 1.0, 0.0).astype(BF16)
        summed = dot(selector, msg[...]).astype(BF16)
        hidden = silu(pre_node[here, :] + dot(summed, nw[0, 1])).astype(BF16)
        output = dot(hidden, nw[0, 2]) + biases[1, 1:2, :]
        updated = layer_norm(output, gains[1:2, :], biases[2, 1:2, :])
        mout[here, :] = (latent[here, :].astype(F32) + updated).astype(BF16)
        halo_copy(0, c).start()
        halo_copy(1, c).start()

    store_mesh = pltpu.make_async_copy(mout, mesh_hbm, out_sem)
    store_mesh.start()

    dec_rows[0:3, :] = dec_send[...]
    dec_cols[...] = jnp.transpose(dec_rows[...])
    for k in range(3):
        dec_geo_rows[0:4, :] = dec_geom[k].astype(F32)
        dec_geo_cols[k] = jnp.transpose(dec_geo_rows[...])
    loads[16].wait()

    @pl.loop(0, grid_rows // CHUNK)
    def _(c):
        here = pl.ds(pl.multiple_of(c * CHUNK, CHUNK), CHUNK)
        latents = grid[here, :]
        pre_grid[here, :] = dot(latents, ew[1, 1]) + biases[0, 2:3, :]
        pre_gnode[here, :] = dot(latents, nw[1, 0]) + biases[0, 3:4, :]
        for k in range(3):
            acc[k, here, :] = dot(
                one_hot(dec_cols[here, k:k + 1], rows, rows), mout[...]).astype(BF16)

    chunks = rows // CHUNK
    early = (chunks - 1) * CHUNK

    def neighbours(column, first, count):
        return (
            dot(one_hot(column, first, count), win[0, first:first + count, :])
            + dot(one_hot(column, 2 * rows + first, count), win[1, first:first + count, :])
        )

    for c in range(early // CHUNK):
        halo_copy(0, c).wait_recv()
        halo_copy(1, c).wait_recv()

    @pl.loop(0, grid_rows // CHUNK)
    def _(c):
        here = pl.ds(pl.multiple_of(c * CHUNK, CHUNK), CHUNK)
        for k in range(3):
            acc[k, here, :] = (
                acc[k, here, :].astype(F32) + neighbours(dec_cols[here, k:k + 1], 0, early)
            ).astype(BF16)

    for c in range(early // CHUNK, chunks):
        halo_copy(0, c).wait_recv()
        halo_copy(1, c).wait_recv()

    def store_grid(c):
        here = pl.ds(pl.multiple_of(c * CHUNK, CHUNK), CHUNK)
        return pltpu.make_async_copy(gout.at[here], grid_out_hbm.at[here], gout_sem.at[c])

    @pl.loop(0, grid_rows // CHUNK)
    def _(c):
        here = pl.ds(pl.multiple_of(c * CHUNK, CHUNK), CHUNK)
        total = jnp.zeros((CHUNK, latent.shape[1]), F32)
        for k in range(3):
            picked = (
                acc[k, here, :].astype(F32)
                + neighbours(dec_cols[here, k:k + 1], early, rows - early)
            ).astype(BF16)
            pre = (
                dot(picked, ew[1, 0]) + pre_grid[here, :]
                + dot(dec_geo_cols[k, here, :].astype(BF16), geom_w[1].astype(BF16))
            )
            output = dot(silu(pre).astype(BF16), ew[1, 2]) + biases[1, 2:3, :]
            total += layer_norm(output, gains[2:3, :], biases[2, 2:3, :])
        hidden = silu(pre_gnode[here, :] + dot(total.astype(BF16), nw[1, 1])).astype(BF16)
        output = dot(hidden, nw[1, 2]) + biases[1, 3:4, :]
        updated = layer_norm(output, gains[3:4, :], biases[2, 3:4, :])
        gout[here, :] = (grid[here, :].astype(F32) + updated).astype(BF16)
        store_grid(c).start()

    for c in range(grid_rows // CHUNK):
        store_grid(c).wait()
    store_mesh.wait()
    for request in requests:
        request.wait_send()
    for reply in replies:
        reply.wait_send()

    @pl.loop(1, n)
    def _(k):
        hot_copy(k).wait_send()

    for c in range(chunks):
        halo_copy(0, c).wait_send()
        halo_copy(1, c).wait_send()


def local(
    mesh_latent, grid_latent, near_senders, near_receivers, near_counts, near_geom,
    far_senders, far_receivers, far_counts, far_geom, dec_senders, dec_geom,
    edge_weights, node_weights, geom_weights, biases, gains,
):
    n = lax.axis_size("lat")
    rows, width = mesh_latent.shape
    grid_rows = grid_latent.shape[0]
    cap = near_senders.shape[2]
    far_cap = far_senders.shape[2]
    caps = ((2, cap), (1, cap // 2), (3, cap // 2), (0, cap // 4), (4, cap // 4))
    edges = sum(c for _, c in caps) + far_cap * (-(-n // 128) * 128)
    remote = sum(c for _, c in caps[1:])
    chunks = rows // CHUNK
    operands = (
        mesh_latent, grid_latent, near_senders.transpose(1, 0, 2), near_receivers.transpose(1, 0, 2),
        near_counts, near_geom[0], far_senders.transpose(0, 2, 1)[0], far_receivers.transpose(0, 2, 1)[0],
        far_counts, far_geom[0], dec_senders, dec_geom.transpose(1, 0, 2),
        edge_weights, node_weights, geom_weights, biases.transpose(1, 0, 2), gains,
    )

    def like(i):
        return pltpu.VMEM(operands[i].shape, operands[i].dtype)

    hbm = pl.BlockSpec(memory_space=pl.ANY)
    dma = pltpu.SemaphoreType.DMA
    return pl.pallas_call(
        functools.partial(kernel, n, caps, far_cap),
        out_shape=(
            jax.ShapeDtypeStruct((rows, width), BF16),
            jax.ShapeDtypeStruct((grid_rows, width), BF16),
        ),
        in_specs=[hbm] * len(operands),
        out_specs=(hbm, hbm),
        scratch_shapes=[
            like(0), like(3), like(2), like(4), like(5), like(6), like(7), like(8), like(9),
            like(10), like(11), like(14), like(15), like(16),
            pltpu.VMEM((8, edges), jnp.int32),
            pltpu.VMEM((8, edges), F32),
            pltpu.VMEM((8, grid_rows), jnp.int32),
            pltpu.VMEM((8, grid_rows), F32),
            pltpu.VMEM((2, 8, width), F32),
            like(12), like(13), like(1),
            pltpu.VMEM((4, 5, 1, cap), jnp.int32),
            pltpu.VMEM((remote, width), BF16),
            pltpu.VMEM((remote, width), BF16),
            pltpu.VMEM((n * HOT_ROWS, width), BF16),
            pltpu.VMEM((edges, 8), jnp.int32),
            pltpu.VMEM((edges, 8), F32),
            pltpu.VMEM((grid_rows, 8), jnp.int32),
            pltpu.VMEM((3, grid_rows, 8), F32),
            pltpu.VMEM((edges, width), F32),
            pltpu.VMEM((edges, width), BF16),
            pltpu.VMEM((rows, width), F32),
            pltpu.VMEM((rows, width), BF16),
            pltpu.VMEM((2, rows, width), BF16),
            pltpu.VMEM((3, grid_rows, width), BF16),
            pltpu.VMEM((grid_rows, width), F32),
            pltpu.VMEM((grid_rows, width), F32),
            pltpu.VMEM((grid_rows, width), BF16),
            dma((len(operands),)), dma((4,)), dma((4,)), dma((4,)), dma((4,)), dma((n,)), dma((n,)),
            dma((2, chunks)), dma((2, chunks)), dma, dma((grid_rows // CHUNK,)),
        ],
        compiler_params=pltpu.CompilerParams(
            collective_id=0, has_side_effects=True, vmem_limit_bytes=58 * 2**20,
        ),
        cost_estimate=pl.CostEstimate(
            flops=25_000_000_000, bytes_accessed=12_000_000, transcendentals=4_000_000),
    )(*operands)


def solution(mesh):
    return jax.shard_map(
        local,
        mesh=mesh,
        in_specs=(
            P(("groups", "lat"), None),
            P(("groups", "lat"), None),
            P(("groups", "lat"), None, None),
            P(("groups", "lat"), None, None),
            P(("groups", "lat"), None),
            P(("groups", "lat"), None, None),
            P(("groups", "lat"), None, None),
            P(("groups", "lat"), None, None),
            P(("groups", "lat"), None),
            P(("groups", "lat"), None, None),
            P(None, ("groups", "lat")),
            P(None, None, ("groups", "lat")),
            P(),
            P(),
            P(),
            P(),
            P(),
        ),
        out_specs=(P(("groups", "lat"), None), P(("groups", "lat"), None)),
        check_vma=False,
    )
```

```python
import functools

import jax
import jax.numpy as jnp
from jax import lax
from jax.experimental import pallas as pl
from jax.experimental.pallas import tpu as pltpu
from jax.sharding import PartitionSpec as P

EPSILON = 1e-05
MESH = pl.DeviceIdType.MESH
F32 = jnp.float32
BF16 = jnp.bfloat16
CHUNK = 256
HOT_ROWS = 16


def dot(left, right):
    return jnp.dot(left, right, preferred_element_type=F32)


def silu(value):
    half = 0.5 * value
    return half + half * jnp.tanh(half)


def layer_norm(values, gain, shift):
    average = jnp.mean(values, axis=-1, keepdims=True)
    centred = values - average
    variance = jnp.mean(centred * centred, axis=-1, keepdims=True)
    return centred * lax.rsqrt(variance + EPSILON) * gain + shift


def one_hot(column, first, count):
    ids = lax.broadcasted_iota(jnp.int32, (column.shape[0], count), 1) + first
    return jnp.where(ids == column, 1.0, 0.0).astype(BF16)


def kernel(
    n, caps, far_cap,
    latent_hbm, grid_hbm, send_hbm, recv_hbm, counts_hbm, geom_hbm,
    far_send_hbm, far_recv_hbm, far_counts_hbm, far_geom_hbm,
    dec_send_hbm, dec_geom_hbm, ew_hbm, nw_hbm, geom_w_hbm, biases_hbm, gains_hbm,
    mesh_hbm, grid_out_hbm,
    latent, near_recv, near_send, counts, near_geom, far_send, far_recv, far_counts, far_geom,
    dec_send, dec_geom, geom_raw, biases, gains,
    idx_rows, geo_rows, dec_rows, dec_geo_rows, geom_w,
    ew, nw, grid, idx_in, served, sent, hot, cols, geo_cols, dec_cols, dec_geo_cols,
    pre_edge, msg, pre_node, mout, win, acc, pre_grid, pre_gnode, gout,
    load_sem, idx_send, idx_recv, row_send, row_recv, hot_send, hot_recv,
    halo_send, halo_recv, out_sem, gout_sem,
):
    me = lax.axis_index("lat")
    rows = latent.shape[0]
    grid_rows = grid.shape[0]
    edges = idx_rows.shape[1]
    near_edges = sum(cap for _, cap in caps)
    own = caps[0][1]
    far_edges = edges - near_edges

    def peer(by):
        return {"lat": lax.rem(me + by + 2 * n, n)}

    barrier = pltpu.get_barrier_semaphore()

    @pl.loop(1, n)
    def _(k):
        pl.semaphore_signal(barrier, inc=1, device_id=peer(k), device_id_type=MESH)

    pairs = (
        (latent_hbm, latent), (send_hbm, near_send), (recv_hbm, near_recv), (counts_hbm, counts),
        (geom_hbm, near_geom), (far_send_hbm, far_send), (far_recv_hbm, far_recv),
        (far_counts_hbm, far_counts), (far_geom_hbm, far_geom), (dec_send_hbm, dec_send),
        (dec_geom_hbm, dec_geom), (geom_w_hbm, geom_raw), (biases_hbm, biases), (gains_hbm, gains),
        (ew_hbm, ew), (nw_hbm, nw), (grid_hbm, grid),
    )
    loads = [
        pltpu.make_async_copy(source, target, load_sem.at[i])
        for i, (source, target) in enumerate(pairs)
    ]
    for load in loads:
        load.start()

    starts, at = ({}, 0)
    for j, cap in caps:
        starts[j] = at
        at += cap
    pl.semaphore_wait(barrier, n - 1)

    requests = []
    for slot, (j, cap) in enumerate(caps[1:]):
        requests.append(pltpu.make_async_remote_copy(
            src_ref=send_hbm, dst_ref=idx_in.at[slot],
            send_sem=idx_send.at[slot], recv_sem=idx_recv.at[slot],
            device_id=peer(j - 2), device_id_type=MESH,
        ))
        requests[-1].start()

    def hot_copy(k):
        return pltpu.make_async_remote_copy(
            src_ref=latent_hbm.at[pl.ds(0, HOT_ROWS)],
            dst_ref=hot.at[pl.ds(pl.multiple_of(me * HOT_ROWS, HOT_ROWS), HOT_ROWS)],
            send_sem=hot_send.at[k], recv_sem=hot_recv.at[k],
            device_id=peer(k), device_id_type=MESH,
        )

    @pl.loop(1, n)
    def _(k):
        hot_copy(k).start()

    loads[0].wait()

    replies = []
    for slot, (j, cap) in enumerate(caps[1:]):
        requests[slot].wait_recv()
        wanted = jnp.transpose(jnp.broadcast_to(idx_in[slot, j, :, :cap], (8, cap)))
        place = starts[j] - own
        served[place:place + cap, :] = dot(
            one_hot(wanted[:, 0:1], 0, rows), latent[...]).astype(BF16)
        replies.append(pltpu.make_async_remote_copy(
            src_ref=served.at[pl.ds(place, cap)],
            dst_ref=sent.at[pl.ds(place, cap)],
            send_sem=row_send.at[slot], recv_sem=row_recv.at[slot],
            device_id=peer(2 - j), device_id_type=MESH,
        ))
        replies[-1].start()

    idx_rows[...] = jnp.zeros_like(idx_rows)
    idx_rows[2:3, :] = jnp.full((1, edges), -1, jnp.int32)
    geo_rows[...] = jnp.zeros_like(geo_rows)
    dec_rows[...] = jnp.zeros_like(dec_rows)
    dec_geo_rows[...] = jnp.zeros_like(dec_geo_rows)
    geom_w[...] = jnp.zeros_like(geom_w)
    for load in loads[1:14]:
        load.wait()
    hot[pl.ds(pl.multiple_of(me * HOT_ROWS, HOT_ROWS), HOT_ROWS), :] = latent[0:HOT_ROWS, :]

    for j, cap in caps:
        here = slice(starts[j], starts[j] + cap)
        to = near_recv[j, :, :cap]
        live = lax.broadcasted_iota(jnp.int32, (1, cap), 1) < counts[0:1, j:j + 1]
        idx_rows[0:1, here] = to
        idx_rows[1:2, here] = near_send[j, :, :cap]
        idx_rows[2:3, here] = jnp.where(live, to, -1)
        first = j * near_recv.shape[2]
        geo_rows[0:4, here] = near_geom[:, first:first + cap].astype(F32)
    wide = far_edges // far_cap
    for c in range(far_cap):
        first = near_edges + c * wide
        here = slice(first, first + n)
        to = far_recv[c:c + 1, :]
        idx_rows[0:1, here] = to
        idx_rows[1:2, here] = far_send[c:c + 1, :] + HOT_ROWS * lax.broadcasted_iota(jnp.int32, (1, n), 1)
        idx_rows[2:3, here] = jnp.where(far_counts[0:1, :] > c, to, -1)
        place = lax.broadcasted_iota(jnp.int32, (far_cap * n, wide), 0)
        slots = far_cap * lax.broadcasted_iota(jnp.int32, (far_cap * n, wide), 1) + c
        geo_rows[0:4, first:first + wide] = dot(
            far_geom[...], jnp.where(place == slots, 1.0, 0.0).astype(BF16))
    geom_w[:, 0:4, :] = geom_raw[...].astype(F32)
    cols[...] = jnp.transpose(idx_rows[...])
    geo_cols[...] = jnp.transpose(geo_rows[...])

    loads[14].wait()
    loads[15].wait()

    def received(start, count):
        here = pl.ds(start, count)
        picked = dot(one_hot(cols[here, 0:1], 0, rows), latent[...]).astype(BF16)
        pre_edge[here, :] = (
            dot(picked, ew[0, 1])
            + dot(geo_cols[here, :].astype(BF16), geom_w[0].astype(BF16))
            + biases[0, 0:1, :]
        )

    def message(sent_rows, start, count):
        here = pl.ds(start, count)
        hidden = silu(dot(sent_rows, ew[0, 0]) + pre_edge[here, :]).astype(BF16)
        output = dot(hidden, ew[0, 2]) + biases[1, 0:1, :]
        msg[here, :] = layer_norm(output, gains[0:1, :], biases[2, 0:1, :]).astype(BF16)

    @pl.loop(0, near_edges // CHUNK)
    def _(c):
        received(pl.multiple_of(c * CHUNK, CHUNK), CHUNK)

    received(near_edges, far_edges)

    @pl.loop(0, own // CHUNK)
    def _(c):
        start = pl.multiple_of(c * CHUNK, CHUNK)
        picked = dot(one_hot(cols[pl.ds(start, CHUNK), 1:2], 0, rows), latent[...])
        message(picked.astype(BF16), start, CHUNK)

    @pl.loop(0, rows // CHUNK)
    def _(c):
        here = pl.ds(pl.multiple_of(c * CHUNK, CHUNK), CHUNK)
        pre_node[here, :] = dot(latent[here, :], nw[0, 0]) + biases[0, 1:2, :]

    @pl.loop(1, n)
    def _(k):
        hot_copy(k).wait_recv()

    hot_rows = dot(one_hot(cols[near_edges:edges, 1:2], 0, n * HOT_ROWS), hot[...])
    message(hot_rows.astype(BF16), near_edges, far_edges)

    for reply in replies:
        reply.wait_recv()

    @pl.loop(0, (near_edges - own) // CHUNK)
    def _(c):
        start = pl.multiple_of(c * CHUNK, CHUNK)
        message(sent[pl.ds(start, CHUNK), :], pl.multiple_of(own + start, CHUNK), CHUNK)

    def halo_copy(side, c):
        here = pl.ds(pl.multiple_of(c * CHUNK, CHUNK), CHUNK)
        return pltpu.make_async_remote_copy(
            src_ref=mout.at[here], dst_ref=win.at[side, here],
            send_sem=halo_send.at[side, c], recv_sem=halo_recv.at[side, c],
            device_id=peer(1 - 2 * side), device_id_type=MESH,
        )

    quick = 1 - lax.rem(me, 2)
    slow = 1 - quick

    @pl.loop(0, rows // CHUNK)
    def _(c):
        first = pl.multiple_of(c * CHUNK, CHUNK)
        here = pl.ds(first, CHUNK)
        ids = lax.broadcasted_iota(jnp.int32, (CHUNK, edges), 0) + first
        selector = jnp.where(ids == idx_rows[2:3, :], 1.0, 0.0).astype(BF16)
        summed = dot(selector, msg[...]).astype(BF16)
        hidden = silu(pre_node[here, :] + dot(summed, nw[0, 1])).astype(BF16)
        output = dot(hidden, nw[0, 2]) + biases[1, 1:2, :]
        updated = layer_norm(output, gains[1:2, :], biases[2, 1:2, :])
        mout[here, :] = (latent[here, :].astype(F32) + updated).astype(BF16)
        halo_copy(quick, c).start()
        halo_copy(slow, c).start()

    store_mesh = pltpu.make_async_copy(mout, mesh_hbm, out_sem)
    store_mesh.start()

    dec_rows[0:3, :] = dec_send[...]
    dec_cols[...] = jnp.transpose(dec_rows[...])
    for k in range(3):
        dec_geo_rows[0:4, :] = dec_geom[k].astype(F32)
        dec_geo_cols[k] = jnp.transpose(dec_geo_rows[...])
    loads[16].wait()

    @pl.loop(0, grid_rows // CHUNK)
    def _(c):
        here = pl.ds(pl.multiple_of(c * CHUNK, CHUNK), CHUNK)
        latents = grid[here, :]
        pre_grid[here, :] = dot(latents, ew[1, 1]) + biases[0, 2:3, :]
        pre_gnode[here, :] = dot(latents, nw[1, 0]) + biases[0, 3:4, :]

    chunks = rows // CHUNK

    def from_side(side, column, first, count):
        offset = side * 2 * rows + first
        return dot(one_hot(column, offset, count), win[side, first:first + count, :])

    for c in range(chunks):
        halo_copy(quick, c).wait_recv()

    @pl.loop(0, grid_rows // CHUNK)
    def _(c):
        here = pl.ds(pl.multiple_of(c * CHUNK, CHUNK), CHUNK)
        for k in range(3):
            column = dec_cols[here, k:k + 1]
            acc[k, here, :] = (
                dot(one_hot(column, rows, rows), mout[...]) + from_side(quick, column, 0, rows)
            ).astype(BF16)

    early = (chunks - 1) * CHUNK
    middle = early // CHUNK // 2 * CHUNK
    for first, last in ((0, middle), (middle, early)):
        for c in range(first // CHUNK, last // CHUNK):
            halo_copy(slow, c).wait_recv()

        @pl.loop(0, grid_rows // CHUNK)
        def _(c, first=first, last=last):
            here = pl.ds(pl.multiple_of(c * CHUNK, CHUNK), CHUNK)
            for k in range(3):
                acc[k, here, :] = (
                    acc[k, here, :].astype(F32)
                    + from_side(slow, dec_cols[here, k:k + 1], first, last - first)
                ).astype(BF16)

    for c in range(early // CHUNK, chunks):
        halo_copy(slow, c).wait_recv()

    def store_grid(c):
        here = pl.ds(pl.multiple_of(c * CHUNK, CHUNK), CHUNK)
        return pltpu.make_async_copy(gout.at[here], grid_out_hbm.at[here], gout_sem.at[c])

    @pl.loop(0, grid_rows // CHUNK)
    def _(c):
        here = pl.ds(pl.multiple_of(c * CHUNK, CHUNK), CHUNK)
        total = jnp.zeros((CHUNK, latent.shape[1]), F32)
        for k in range(3):
            picked = (
                acc[k, here, :].astype(F32)
                + from_side(slow, dec_cols[here, k:k + 1], early, rows - early)
            ).astype(BF16)
            pre = (
                dot(picked, ew[1, 0]) + pre_grid[here, :]
                + dot(dec_geo_cols[k, here, :].astype(BF16), geom_w[1].astype(BF16))
            )
            output = dot(silu(pre).astype(BF16), ew[1, 2]) + biases[1, 2:3, :]
            total += layer_norm(output, gains[2:3, :], biases[2, 2:3, :])
        hidden = silu(pre_gnode[here, :] + dot(total.astype(BF16), nw[1, 1])).astype(BF16)
        output = dot(hidden, nw[1, 2]) + biases[1, 3:4, :]
        updated = layer_norm(output, gains[3:4, :], biases[2, 3:4, :])
        gout[here, :] = (grid[here, :].astype(F32) + updated).astype(BF16)
        store_grid(c).start()

    for c in range(grid_rows // CHUNK):
        store_grid(c).wait()
    store_mesh.wait()
    for request in requests:
        request.wait_send()
    for reply in replies:
        reply.wait_send()

    @pl.loop(1, n)
    def _(k):
        hot_copy(k).wait_send()

    for c in range(chunks):
        halo_copy(0, c).wait_send()
        halo_copy(1, c).wait_send()


def local(
    mesh_latent, grid_latent, near_senders, near_receivers, near_counts, near_geom,
    far_senders, far_receivers, far_counts, far_geom, dec_senders, dec_geom,
    edge_weights, node_weights, geom_weights, biases, gains,
):
    n = lax.axis_size("lat")
    rows, width = mesh_latent.shape
    grid_rows = grid_latent.shape[0]
    cap = near_senders.shape[2]
    far_cap = far_senders.shape[2]
    caps = ((2, cap), (1, cap // 2), (3, cap // 2), (0, cap // 4), (4, cap // 4))
    edges = sum(c for _, c in caps) + far_cap * (-(-n // 128) * 128)
    remote = sum(c for _, c in caps[1:])
    chunks = rows // CHUNK
    operands = (
        mesh_latent, grid_latent, near_senders.transpose(1, 0, 2), near_receivers.transpose(1, 0, 2),
        near_counts, near_geom[0], far_senders.transpose(0, 2, 1)[0], far_receivers.transpose(0, 2, 1)[0],
        far_counts, far_geom[0], dec_senders, dec_geom.transpose(1, 0, 2),
        edge_weights, node_weights, geom_weights, biases.transpose(1, 0, 2), gains,
    )

    def like(i):
        return pltpu.VMEM(operands[i].shape, operands[i].dtype)

    hbm = pl.BlockSpec(memory_space=pl.ANY)
    dma = pltpu.SemaphoreType.DMA
    return pl.pallas_call(
        functools.partial(kernel, n, caps, far_cap),
        out_shape=(
            jax.ShapeDtypeStruct((rows, width), BF16),
            jax.ShapeDtypeStruct((grid_rows, width), BF16),
        ),
        in_specs=[hbm] * len(operands),
        out_specs=(hbm, hbm),
        scratch_shapes=[
            like(0), like(3), like(2), like(4), like(5), like(6), like(7), like(8), like(9),
            like(10), like(11), like(14), like(15), like(16),
            pltpu.VMEM((8, edges), jnp.int32),
            pltpu.VMEM((8, edges), F32),
            pltpu.VMEM((8, grid_rows), jnp.int32),
            pltpu.VMEM((8, grid_rows), F32),
            pltpu.VMEM((2, 8, width), F32),
            like(12), like(13), like(1),
            pltpu.VMEM((4, 5, 1, cap), jnp.int32),
            pltpu.VMEM((remote, width), BF16),
            pltpu.VMEM((remote, width), BF16),
            pltpu.VMEM((n * HOT_ROWS, width), BF16),
            pltpu.VMEM((edges, 8), jnp.int32),
            pltpu.VMEM((edges, 8), F32),
            pltpu.VMEM((grid_rows, 8), jnp.int32),
            pltpu.VMEM((3, grid_rows, 8), F32),
            pltpu.VMEM((edges, width), F32),
            pltpu.VMEM((edges, width), BF16),
            pltpu.VMEM((rows, width), F32),
            pltpu.VMEM((rows, width), BF16),
            pltpu.VMEM((2, rows, width), BF16),
            pltpu.VMEM((3, grid_rows, width), BF16),
            pltpu.VMEM((grid_rows, width), F32),
            pltpu.VMEM((grid_rows, width), F32),
            pltpu.VMEM((grid_rows, width), BF16),
            dma((len(operands),)), dma((4,)), dma((4,)), dma((4,)), dma((4,)), dma((n,)), dma((n,)),
            dma((2, chunks)), dma((2, chunks)), dma, dma((grid_rows // CHUNK,)),
        ],
        compiler_params=pltpu.CompilerParams(
            collective_id=0, has_side_effects=True, vmem_limit_bytes=58 * 2**20,
        ),
        cost_estimate=pl.CostEstimate(
            flops=25_000_000_000, bytes_accessed=12_000_000, transcendentals=4_000_000),
    )(*operands)


def solution(mesh):
    return jax.shard_map(
        local,
        mesh=mesh,
        in_specs=(
            P(("groups", "lat"), None),
            P(("groups", "lat"), None),
            P(("groups", "lat"), None, None),
            P(("groups", "lat"), None, None),
            P(("groups", "lat"), None),
            P(("groups", "lat"), None, None),
            P(("groups", "lat"), None, None),
            P(("groups", "lat"), None, None),
            P(("groups", "lat"), None),
            P(("groups", "lat"), None, None),
            P(None, ("groups", "lat")),
            P(None, None, ("groups", "lat")),
            P(),
            P(),
            P(),
            P(),
            P(),
        ),
        out_specs=(P(("groups", "lat"), None), P(("groups", "lat"), None)),
        check_vma=False,
    )
```
